512 devices in a mesh: var: 64 (over y, x, z_lo), head: 8 (over z_hi, core).
Axes of the slice: x: 4, y: 8, z: 8 (z_hi: 4, z_lo: 2; z = z_hi * 2 + z_lo), core: 2. Of those that a mesh axis runs over, the one named last changes fastest.
Arguments:
- series: float32 [8192, 8192], P('var', 'head'), may hold values from -48 to 48
- emb_weight: float32 [8192, 512], P('head'), as said below
- emb_bias: float32 [512], replicated, may hold values from -3 to 3
- q_weight: float32 [512, 512], P(None, 'head'), may hold values from -0.75 to 0.75
- k_weight: float32 [512, 512], P(None, 'head'), may hold values from -0.25 to 0.25
- v_weight: float32 [512, 512], P(None, 'head'), may hold values from -0.25 to 0.25
- out_weight: float32 [512, 512], P('head'), may hold values from -0.25 to 0.25
- norm1_gain: float32 [512], replicated, may hold values from 0.1 to 1.9
- norm1_bias: float32 [512], replicated, may hold values from -3 to 3
- ffn_in: float32 [512, 2048], P(None, 'head'), may hold values from -0.25 to 0.25
- ffn_out: float32 [2048, 512], P('head'), may hold values from -0.1875 to 0.1875
- norm2_gain: float32 [512], replicated, may hold values from 0.1 to 1.9
- norm2_bias: float32 [512], replicated, may hold values from -3 to 3
Outputs:
- final: float32 [512, 8192], P('head', 'var')
The draws below stay inside these ranges and needn't reach their ends.
Inputs may be any that keep to these rules, and one draw needn't show every extreme that they name: `emb_weight`: every entry lies within 12 / sqrt(8192) in magnitude, and some entry reaches that bound.
All inputs are finite; a program needn't handle non-finite values.
Results may differ from the reference program's by a relative error of at most 0.0003.
Values sent between devices are 32-bit elements; how exact they have to be, the bound alone decides.
A program may use at most 64 MiB of HBM per device.

```python
import math
import jax
import jax.numpy as jnp
from jax import lax

D = 512
FF = 2048
H = 8
L = 8192
DH = 64
VARS = 8192


def draw_series(key, part):
    base = jnp.clip(jax.random.normal(jax.random.fold_in(key, 11), (VARS, L), jnp.float32), -6.0, 6.0)
    base = base.at[0, 0].set(6.0)
    return base


def draw_emb_weight(key, part):
    base = jnp.clip(jax.random.normal(jax.random.fold_in(key, 21), (L, D), jnp.float32), -4.0, 4.0)
    base = base.at[0, D - 1].set(4.0)
    column_scale = jnp.exp(jnp.linspace(math.log(0.4), math.log(3.0), D, dtype=jnp.float32))
    return base * column_scale[None, :] / math.sqrt(L)


def with_spikes(values, own_key, source, target, parts, factor):
    def block_of(axis_at):
        return (jnp.arange(values.shape[axis_at]) // (values.shape[axis_at] // parts)).reshape((-1,) + (1,) * (values.ndim - 1 - axis_at))

    one_side = jax.random.permutation(own_key, parts)[block_of(target)]
    far = (block_of(target) + parts // 2) % parts
    return jnp.where((block_of(source) == one_side) | (block_of(source) == far), factor * values, values)


def level_of(stream_key, dims, cuts, smallest, high):
    factor_of = 1.0
    for axis_at, shards_of in cuts:
        steps = jax.random.uniform(jax.random.fold_in(jax.random.fold_in(stream_key, 6), axis_at), (shards_of,), jnp.float32, smallest / len(cuts), high / len(cuts))
        factor_of = factor_of * jnp.repeat(jnp.exp(steps), dims[axis_at] // shards_of).reshape((-1,) + (1,) * (len(dims) - 1 - axis_at))
    return factor_of


def bell_draw(own_key, shape, scale, bound, pieces=(), held_as=jnp.bfloat16):
    values = scale * jax.random.normal(own_key, shape, jnp.float32)
    if pieces:
        values = values * level_of(own_key, shape, pieces, -0.22, 0.18)
    return jnp.clip(values, -bound, bound).astype(held_as)


def gaussian_with(rng, shape, scale, reach, cuts, heavy, kind=jnp.bfloat16):
    drawn = scale * jax.random.normal(rng, shape, jnp.float32)
    if cuts:
        drawn = drawn * level_of(rng, shape, cuts, -0.22, 0.18)
    return jnp.clip(with_spikes(drawn, jax.random.fold_in(rng, 3), *heavy), -reach, reach).astype(kind)


def setup_inputs(seed: int = 0) -> dict:
    streams_of = jax.random.split(jax.random.key(seed), 14)
    return {
        "series": draw_series(jax.random.fold_in(streams_of[13], 71), 0),
        "emb_weight": draw_emb_weight(jax.random.fold_in(streams_of[13], 71), 0),
        "emb_bias": bell_draw(streams_of[2], (D,), 0.5, 3.0, (), jnp.float32),
        "q_weight": bell_draw(streams_of[3], (D, D), (D // 9) ** -0.5, 0.75, ((1, 8),), jnp.float32),
        "k_weight": bell_draw(streams_of[4], (D, D), D ** -0.5, 0.25, ((1, 8),), jnp.float32),
        "v_weight": bell_draw(streams_of[5], (D, D), D ** -0.5, 0.25, ((1, 8),), jnp.float32),
        "out_weight": bell_draw(streams_of[6], (D, D), D ** -0.5, 0.25, ((0, 8),), jnp.float32),
        "norm1_gain": jnp.clip(1.0 + 0.18 * jax.random.normal(streams_of[7], (D,), jnp.float32), 0.1, 1.9),
        "norm1_bias": bell_draw(streams_of[8], (D,), 0.5, 3.0, (), jnp.float32),
        "ffn_in": bell_draw(streams_of[9], (D, FF), D ** -0.5, 0.25, ((1, 8),), jnp.float32),
        "ffn_out": gaussian_with(streams_of[10], (FF, D), FF ** -0.5, 0.1875, ((0, 8),), (0, 1, 8, 2.0), jnp.float32),
        "norm2_gain": jnp.clip(1.0 + 0.18 * jax.random.normal(streams_of[11], (D,), jnp.float32), 0.1, 1.9),
        "norm2_bias": bell_draw(streams_of[12], (D,), 0.5, 3.0, (), jnp.float32),
    }


HIGH = lax.Precision.HIGHEST

def product(first_op, second_op):
    return jnp.dot(first_op, second_op, precision=HIGH, preferred_element_type=jnp.float32)

def layer_norm(stream, scale_gain, shift_bias):
    centre = lax.optimization_barrier(jnp.mean(stream, axis=-1, keepdims=True))
    spread = stream - centre
    variance = lax.optimization_barrier(jnp.mean(spread * spread, axis=-1, keepdims=True))
    return spread * lax.rsqrt(variance + 1e-05) * scale_gain + shift_bias

def reference(series, emb_weight, emb_bias, q_weight, k_weight, v_weight, out_weight, norm1_gain, norm1_bias, ffn_in, ffn_out, norm2_gain, norm2_bias):
    embedded = product(series, emb_weight) + emb_bias
    queries = product(embedded, q_weight).reshape(VARS, H, DH).transpose(1, 0, 2)
    key_rows = product(embedded, k_weight).reshape(VARS, H, DH).transpose(1, 0, 2)
    values = product(embedded, v_weight).reshape(VARS, H, DH).transpose(1, 0, 2)
    block_len = math.gcd(VARS, 1024)
    score_scale = 1.0 / math.sqrt(DH)

    def one_head(operands):
        head_q, head_k, head_v = operands
        blocks = head_q.reshape(VARS // block_len, block_len, DH)

        def one_block(query_block):
            scores = lax.dot_general(query_block, head_k, (((1,), (1,)), ((), ())), precision=HIGH, preferred_element_type=jnp.float32) * score_scale
            row_max = lax.optimization_barrier(jnp.max(scores, axis=1, keepdims=True))
            weights = jnp.exp(scores - row_max)
            return product(weights, head_v) / lax.optimization_barrier(jnp.sum(weights, axis=1, keepdims=True))
        return lax.map(one_block, blocks).reshape(VARS, DH)
    mixed_rows = lax.map(one_head, (queries, key_rows, values))
    mixed_rows = mixed_rows.transpose(1, 0, 2).reshape(VARS, D)
    normed = layer_norm(embedded + product(mixed_rows, out_weight), norm1_gain, norm1_bias)
    hidden = jax.nn.gelu(product(normed, ffn_in), approximate=False)
    result_rows = layer_norm(normed + product(hidden, ffn_out), norm2_gain, norm2_bias)
    return result_rows.T
```

```python
import functools
import math

import jax
import jax.numpy as jnp
from jax import lax
from jax.experimental import pallas as pl
from jax.experimental.pallas import tpu as pltpu
from jax.sharding import PartitionSpec as P

MESH = pl.DeviceIdType.MESH
F32 = jnp.float32
BF16 = jnp.bfloat16

D = 512
FF_PART = 256
DH = 64
ROWS = 128
NY, NX, NZL, NZH, NC = 8, 4, 2, 4, 2
NHEAD = NZH * NC
Z_OFFS = (2, 1, 3)
Y_ORDER = (4, 3, 5, 2, 6, 1, 7, 0)
KV_OFFS = ((2, 1), (2, 0), (1, 1), (3, 1), (1, 0), (3, 0), (0, 1))
COPIES = 96
EPS = 1e-05


def halves(x):
    top = x.astype(BF16)
    return top, (x - top.astype(F32)).astype(BF16)


def mxu(a, b):
    return lax.dot_general(a, b, (((1,), (0,)), ((), ())), preferred_element_type=F32)


def quads(r, m, n):
    return r[:m, :n] + ((r[:m, n:] + r[m:, :n]) + r[m:, n:])


def side_by_side(x):
    return jnp.concatenate(halves(x), axis=1)


def stacked(x):
    return jnp.concatenate(halves(x), axis=0)


def column(row):
    return jnp.broadcast_to(row, (128, 128)).T


def layer_kernel(
    series_h, ew_h, eb_h, qw_h, kw_h, vw_h, ow_h, n1g_h, n1b_h, fi_h, fo_h, n2g_h, n2b_h,
    out_ref,
    series, ew, qw, kw, vw, ow, fi, fo, vec,
    wqkv, fit, fot, wot, gath, n1g, n1b, own_vec,
    epart, cbuf, sbuf, rsbuf, efull,
    qsend, ksend, vsend, qbuf, kbuf, vbuf, kst, qst, vst,
    osend, obuf, mfull, normed_ref,
    fpart, fcbuf, fsbuf, frsbuf, stat, statbuf,
    lsem, ssem, rsem,
):
    v = lax.axis_index("var")
    h = lax.axis_index("head")
    y, x, zl = v // (NX * NZL), (v // NZL) % NX, v % NZL
    zh, c = h // NC, h % NC
    oc = 1 - c

    def at(y_, x_, zl_, zh_, c_):
        return ((y_ * NX + x_) * NZL + zl_, zh_ * NC + c_)

    core_dev = at(y, x, zl, zh, oc)
    z_devs = [at(y, x, zl, (zh + off) % NZH, c) for off in Z_OFFS]
    x_devs = [at(y, (x + off) % NX, zl, zh, c) for off in (2, 1, 3)]
    head_devs = [(v, (h + off) % NHEAD) for off in range(1, NHEAD)]
    y_to = {off: at((y + off) % NY, x, zl, zh, c) for off in range(1, NY)}
    y_from = {off: at((y + NY - off) % NY, x, zl, zh, c) for off in range(1, NY)}
    kv_devs = [at(y, (x + dx) % NX, (zl + dz) % NZL, zh, c) for dx, dz in KV_OFFS]

    count = [0]
    pending = []

    def send(src, dst, dev):
        i = count[0]
        count[0] += 1
        cp = pltpu.make_async_remote_copy(
            src_ref=src, dst_ref=dst, send_sem=ssem.at[i], recv_sem=rsem.at[i],
            device_id=dev, device_id_type=MESH,
        )
        cp.start()
        pending.append(cp)
        return cp

    def drain():
        while pending:
            pending.pop(0).wait_send()

    lcount = [0]

    def load(src, dst):
        i = lcount[0]
        lcount[0] += 1
        cp = pltpu.make_async_copy(src, dst, lsem.at[i])
        cp.start()
        return cp

    ld_series = load(series_h, series)
    z_order = [(zh + off) % NZH for off in Z_OFFS] + [zh]
    ld_ew = [
        load(ew_h.at[:, pl.ds(pl.multiple_of(zz * 128, 128), 128)], ew.at[k])
        for k, zz in enumerate(z_order)
    ]
    ld_ow = load(ow_h, ow)
    ld_vec = [load(r, vec.at[i]) for i, r in enumerate((eb_h, n1g_h, n1b_h, n2g_h, n2b_h))]
    ld_qkv = [load(a, b) for a, b in ((qw_h, qw), (kw_h, kw), (vw_h, vw))]
    ld_ffn = [load(a, b) for a, b in ((fi_h, fi), (fo_h, fo))]

    barrier = pltpu.get_barrier_semaphore()
    greeted = head_devs + [y_to[off] for off in range(1, NY)] + kv_devs
    for dev in greeted:
        pl.semaphore_signal(barrier, inc=1, device_id=dev, device_id_type=MESH)

    ld_series.wait()
    s_stack = stacked(series[...])

    def emb_step(k):
        ld_ew[k].wait()
        r = mxu(s_stack, side_by_side(ew[k]))
        epart[k] = quads(r, ROWS, 128).T.reshape(NC, DH, ROWS)

    emb_step(0)
    ld_ow.wait()
    pl.semaphore_wait(barrier, len(greeted))

    core_cps = [send(epart.at[0, oc], cbuf.at[0], core_dev)]
    xrows = pl.ds(pl.multiple_of(x * 16, 16), 16)
    gath[c, x, zh] = ow[xrows, :]
    w_z = [send(gath.at[c, x, zh], gath.at[c, x, zh], dev) for dev in z_devs]
    emb_step(1)
    core_cps.append(send(epart.at[1, oc], cbuf.at[1], core_dev))
    z_cps = []

    def to_chip(k):
        core_cps[k].wait_recv()
        sbuf[k] = epart[k, c] + cbuf[k]
        if k < 3:
            z_cps.append(send(sbuf.at[k], rsbuf.at[k], z_devs[k]))

    to_chip(0)
    emb_step(2)
    core_cps.append(send(epart.at[2, oc], cbuf.at[2], core_dev))
    to_chip(1)
    emb_step(3)
    core_cps.append(send(epart.at[3, oc], cbuf.at[3], core_dev))
    to_chip(2)
    to_chip(3)

    for ld in ld_vec + ld_qkv:
        ld.wait()
    kt = kw[...].T
    wqkv[...] = stacked(jnp.concatenate([qw[...].T, vw[...].T, kt, kt], axis=0))
    for i, j in enumerate((0, 3, 4)):
        own_vec[i] = column(vec[j, pl.ds(zh, 1), :]).reshape(NC, DH, ROWS)
    for cp in w_z:
        cp.wait_recv()
    w_x = [send(gath.at[c, x], gath.at[c, x], dev) for dev in x_devs]

    for cp in z_cps:
        cp.wait_recv()
    efull[h] = (sbuf[3] + rsbuf[1]) + (rsbuf[0] + rsbuf[2]) + own_vec[0, c]

    def gather_heads(buf, meanwhile):
        zs = [send(buf.at[h], buf.at[h], dev) for dev in z_devs]
        cs = [send(buf.at[h], buf.at[h], core_dev)]
        meanwhile()
        for k in (1, 2, 0):
            zs[k].wait_recv()
            hs = ((zh + NZH - Z_OFFS[k]) % NZH) * NC + c
            cs.append(send(buf.at[hs], buf.at[hs], core_dev))
        for cp in cs:
            cp.wait_recv()

    def prepare_ffn_in():
        ld_ffn[0].wait()
        fit[...] = stacked(fi[...].T)

    gather_heads(efull, prepare_ffn_in)

    emb_t = efull[...].reshape(D, ROWS)
    qkv = quads(mxu(wqkv[...], side_by_side(emb_t)), 4 * DH, ROWS)
    qsend[...] = qkv[:DH] * (math.log2(math.e) / math.sqrt(DH))
    kk = qkv[2 * DH :].T
    left = lax.broadcasted_iota(jnp.int32, (DH, 128), 1) < DH
    ksend[...] = jnp.where(left, kk[:DH], kk[DH:])
    vsend[...] = qkv[DH : 2 * DH]

    q_cps, k_cps, v_cps = {}, [], []
    for i in range(7):
        off = Y_ORDER[i]
        k_cps.append(send(ksend, kbuf.at[i], kv_devs[i]))
        q_cps[off] = send(qsend, qbuf.at[off], y_to[off])
    for i in range(7):
        v_cps.append(send(vsend, vbuf.at[i], kv_devs[i]))

    for cp in w_x:
        cp.wait_recv()
    w_c = send(gath.at[c], gath.at[c], core_dev)
    ld_ffn[1].wait()
    for z in range(NZH):
        fot[z] = stacked(fo[:, z * 128 : (z + 1) * 128].T)
        n1g[pl.ds(z * 128, 128), :] = column(vec[1, z : z + 1, :])
        n1b[pl.ds(z * 128, 128), :] = column(vec[2, z : z + 1, :])
    w_c.wait_recv()
    for z in range(NZH):
        block = jnp.concatenate(
            [gath[par, xx, z] for par in range(NC) for xx in range(NX)], axis=0
        )
        top, rest = halves(block.T)
        wot[:D, z * 128 : (z + 1) * 128] = top
        wot[D:, z * 128 : (z + 1) * 128] = rest

    def put_key(i, pack):
        other = pltpu.roll(pack, DH, 1)
        for j, kd in enumerate((jnp.where(left, pack, other), jnp.where(left, other, pack))):
            top, rest = halves(kd)
            rows = slice(i * ROWS + j * DH, i * ROWS + (j + 1) * DH)
            kst[rows, :128] = top
            kst[rows, 128:] = rest

    def put_query(j, qt):
        top, rest = halves(qt)
        cols = slice(j * ROWS, (j + 1) * ROWS)
        for r in range(2):
            qst[2 * r * DH : (2 * r + 1) * DH, cols] = top
            qst[(2 * r + 1) * DH : (2 * r + 2) * DH, cols] = rest

    def put_value(i, vt):
        vst[:, i * ROWS : (i + 1) * ROWS] = stacked(vt)

    put_key(7, ksend[...])
    put_value(7, vsend[...])
    put_query(7, qsend[...])
    for i in range(7):
        k_cps[i].wait_recv()
        put_key(i, kbuf[i])
    for i in range(7):
        v_cps[i].wait_recv()
        put_value(i, vbuf[i])

    o_cps = {}
    for pair in range(4):
        for j in (2 * pair, 2 * pair + 1):
            off = Y_ORDER[j]
            if off:
                q_cps[off].wait_recv()
                put_query(j, qbuf[off])
        s = mxu(kst[...], qst[:, 2 * pair * ROWS : (2 * pair + 2) * ROWS])
        top_score = jnp.max(s, axis=0, keepdims=True)
        p = jnp.exp2(s - top_score)
        total = jnp.sum(p, axis=0, keepdims=True)
        p_top, p_rest = halves(p)
        o = mxu(vst[...], p_top) + mxu(vst[...], p_rest)
        o = o[:DH] + o[DH:]
        for j in (2 * pair, 2 * pair + 1):
            off = Y_ORDER[j]
            cols = slice((j % 2) * ROWS, (j % 2 + 1) * ROWS)
            osend[off, :DH] = o[:, cols]
            osend[off, DH : DH + 8] = jnp.concatenate(
                [
                    jnp.broadcast_to(top_score[:, cols], (4, ROWS)),
                    jnp.broadcast_to(total[:, cols], (4, ROWS)),
                ],
                axis=0,
            )
            if off:
                o_cps[off] = send(osend.at[off], obuf.at[off], y_from[off])

    for off in range(1, NY):
        o_cps[off].wait_recv()
    tops = [osend[0, DH : DH + 1]] + [obuf[off, DH : DH + 1] for off in range(1, NY)]
    best = functools.reduce(jnp.maximum, tops)
    scales = [jnp.exp2(t - best) for t in tops]
    denom = scales[0] * osend[0, DH + 4 : DH + 5]
    acc = scales[0] * osend[0, :DH]
    for off in range(1, NY):
        denom += scales[off] * obuf[off, DH + 4 : DH + 5]
        acc += scales[off] * obuf[off, :DH]
    mfull[h] = acc / denom

    gather_heads(mfull, lambda: None)

    mixed_t = mfull[...].reshape(D, ROWS)
    resid = emb_t + quads(mxu(wot[...], side_by_side(mixed_t)), D, ROWS)
    centre = jnp.sum(resid, axis=0, keepdims=True) * (1.0 / D)
    spread = resid - centre
    variance = jnp.sum(spread * spread, axis=0, keepdims=True) * (1.0 / D)
    normed = spread * lax.rsqrt(variance + EPS) * n1g[...] + n1b[...]
    normed_ref[...] = normed.reshape(NHEAD, DH, ROWS)
    hid = quads(mxu(fit[...], side_by_side(normed)), FF_PART, ROWS)
    hid = hid * (1.0 + lax.erf(hid * (1.0 / math.sqrt(2.0)))) * 0.5
    hid2 = side_by_side(hid)

    fcore = []
    for k in range(4):
        fpart[k] = quads(mxu(fot[z_order[k]], hid2), 128, ROWS).reshape(NC, DH, ROWS)
        fcore.append(send(fpart.at[k, oc], fcbuf.at[k], core_dev))
    fz = []
    for k in range(4):
        fcore[k].wait_recv()
        fsbuf[k] = fpart[k, c] + fcbuf[k]
        if k < 3:
            fz.append(send(fsbuf.at[k], frsbuf.at[k], z_devs[k]))
    for cp in fz:
        cp.wait_recv()
    r2 = (fsbuf[3] + frsbuf[1]) + (frsbuf[0] + frsbuf[2]) + normed_ref[h]

    mean_own = jnp.sum(r2, axis=0, keepdims=True) * (1.0 / DH)
    dev_own = r2 - mean_own
    m2_own = jnp.sum(dev_own * dev_own, axis=0, keepdims=True)
    stat[...] = jnp.concatenate(
        [jnp.broadcast_to(mean_own, (4, ROWS)), jnp.broadcast_to(m2_own, (4, ROWS))], axis=0
    )
    st = [send(stat, statbuf.at[i], dev) for i, dev in enumerate(head_devs)]
    for cp in st:
        cp.wait_recv()
    means = [mean_own] + [statbuf[i, 0:1] for i in range(7)]
    mean = functools.reduce(jnp.add, means) * (1.0 / NHEAD)
    m2 = functools.reduce(jnp.add, [m2_own] + [statbuf[i, 4:5] for i in range(7)])
    m2 += DH * functools.reduce(jnp.add, [(m - mean) * (m - mean) for m in means])
    scale = lax.rsqrt(m2 * (1.0 / D) + EPS)
    out_ref[...] = (r2 - mean) * scale * own_vec[1, c] + own_vec[2, c]
    drain()


def on_device(series, emb_weight, emb_bias, q_weight, k_weight, v_weight, out_weight,
              norm1_gain, norm1_bias, ffn_in, ffn_out, norm2_gain, norm2_bias):
    vec4 = lambda a: a.reshape(4, 128)
    vm = lambda *shape: pltpu.VMEM(shape, F32)
    vb = lambda *shape: pltpu.VMEM(shape, BF16)
    block = (DH, ROWS)
    scratch = [
        vm(ROWS, 1024), vm(4, 1024, 128), vm(D, DH), vm(D, DH), vm(D, DH), vm(DH, D),
        vm(D, FF_PART), vm(FF_PART, D), vm(5, 4, 128),
        vb(8 * DH, D), vb(2 * FF_PART, D), vb(4, 256, FF_PART), vb(2 * D, D),
        vm(NC, NX, NZH, 16, D), vm(D, ROWS), vm(D, ROWS), vm(3, NC, *block),
        vm(4, NC, *block), vm(4, *block), vm(4, *block), vm(3, *block), vm(NHEAD, *block),
        vm(*block), vm(*block), vm(*block), vm(NY, *block), vm(7, *block), vm(7, *block),
        vb(1024, 256), vb(256, 1024), vb(128, 1024),
        vm(NY, DH + 8, ROWS), vm(NY, DH + 8, ROWS), vm(NHEAD, *block), vm(NHEAD, *block),
        vm(4, NC, *block), vm(4, *block), vm(4, *block), vm(3, *block),
        vm(8, ROWS), vm(7, 8, ROWS),
        pltpu.SemaphoreType.DMA((16,)), pltpu.SemaphoreType.DMA((COPIES,)),
        pltpu.SemaphoreType.DMA((COPIES,)),
    ]
    return pl.pallas_call(
        layer_kernel,
        out_shape=jax.ShapeDtypeStruct(block, F32),
        in_specs=[pl.BlockSpec(memory_space=pl.ANY)] * 13,
        out_specs=pl.BlockSpec(memory_space=pltpu.VMEM),
        scratch_shapes=scratch,
        compiler_params=pltpu.CompilerParams(
            collective_id=0, has_side_effects=True, vmem_limit_bytes=40 * 1024 * 1024
        ),
        name="layer",
    )(series, emb_weight, vec4(emb_bias), q_weight, k_weight, v_weight, out_weight,
      vec4(norm1_gain), vec4(norm1_bias), ffn_in, ffn_out, vec4(norm2_gain), vec4(norm2_bias))


def solution(mesh):
    return jax.shard_map(
        on_device,
        mesh=mesh,
        in_specs=(
            P("var", "head"), P("head", None), P(), P(None, "head"), P(None, "head"),
            P(None, "head"), P("head", None), P(), P(), P(None, "head"), P("head", None), P(), P(),
        ),
        out_specs=P("head", "var"),
        check_vma=False,
    )
```

```python
import functools
import math

import jax
import jax.numpy as jnp
from jax import lax
from jax.experimental import pallas as pl
from jax.experimental.pallas import tpu as pltpu
from jax.sharding import PartitionSpec as P

MESH = pl.DeviceIdType.MESH
F32 = jnp.float32
BF16 = jnp.bfloat16

D = 512
FF_PART = 256
DH = 64
ROWS = 128
NY, NX, NZL, NZH, NC = 8, 4, 2, 4, 2
NHEAD = NZH * NC
Z_OFFS = (2, 1, 3)
Q_PAIRS = ((0, 1), (7, 2), (6, 3), (5, 4))
KV_OFFS = ((1, 0), (3, 0), (0, 1), (1, 1), (3, 1), (2, 0), (2, 1))
KV_SENDS = (7, 6, 4, 5, 3, 1, 2)
Q_SENDS = (4, 3, 5, 2, 6, 7, 1)
COPIES = 96
EPS = 1e-05


def halves(x):
    top = x.astype(BF16)
    return top, (x - top.astype(F32)).astype(BF16)


def mxu(a, b):
    return lax.dot_general(a, b, (((1,), (0,)), ((), ())), preferred_element_type=F32)


def quads(r, m, n):
    return r[:m, :n] + ((r[:m, n:] + r[m:, :n]) + r[m:, n:])


def side_by_side(x):
    return jnp.concatenate(halves(x), axis=1)


def stacked(x):
    return jnp.concatenate(halves(x), axis=0)


def column(row):
    return jnp.broadcast_to(row, (128, 128)).T


def layer_kernel(
    series_h, ew_h, eb_h, qw_h, kw_h, vw_h, ow_h, n1g_h, n1b_h, fi_h, fo_h, n2g_h, n2b_h,
    out_ref,
    series, ew, qw, kw, vw, ow, fi, fo, vec,
    wqkv, fit, fot, wot, gath, n1g, n1b, own_vec,
    epart, cbuf, sbuf, rsbuf, efull,
    qsend, kvsend, qbuf, kvbuf, kst, qst, vst,
    osend, obuf, mfull, normed_ref,
    fpart, fcbuf, fsbuf, frsbuf, stat, statbuf,
    lsem, ssem, rsem, own_sem,
):
    v = lax.axis_index("var")
    h = lax.axis_index("head")
    y, x, zl = v // (NX * NZL), (v // NZL) % NX, v % NZL
    zh, c = h // NC, h % NC
    oc = 1 - c

    def at(y_, x_, zl_, zh_, c_):
        return ((y_ * NX + x_) * NZL + zl_, zh_ * NC + c_)

    core_dev = at(y, x, zl, zh, oc)
    z_devs = [at(y, x, zl, (zh + off) % NZH, c) for off in Z_OFFS]
    sum_offs = (2, 1 + 2 * zl, 0, 3 - 2 * zl)
    z_order = [(zh + off) % NZH for off in sum_offs]
    sum_devs = [at(y, x, 1 - zl, zz, c) for zz in z_order]
    x_devs = [at(y, (x + off) % NX, zl, zh, c) for off in (2, 1, 3)]
    head_devs = [(v, (h + off) % NHEAD) for off in (4, 3, 5, 2, 6, 7, 1)]
    y_to = {off: at((y + off) % NY, x, zl, zh, c) for off in range(1, NY)}
    y_from = {off: at((y + NY - off) % NY, x, zl, zh, c) for off in range(1, NY)}
    kv_devs = [at(y, (x + dx) % NX, (zl + dz) % NZL, zh, c) for dx, dz in KV_OFFS]

    count = [0]
    pending = []

    def send(src, dst, dev):
        i = count[0]
        count[0] += 1
        cp = pltpu.make_async_remote_copy(
            src_ref=src, dst_ref=dst, send_sem=ssem.at[i], recv_sem=rsem.at[i],
            device_id=dev, device_id_type=MESH,
        )
        cp.start()
        pending.append(cp)
        return cp

    def drain():
        while pending:
            pending.pop(0).wait_send()

    def fence():
        pl.semaphore_signal(own_sem, 1)
        pl.semaphore_wait(own_sem, 1)

    lcount = [0]

    def load(src, dst):
        i = lcount[0]
        lcount[0] += 1
        cp = pltpu.make_async_copy(src, dst, lsem.at[i])
        cp.start()
        return cp

    ld_series = load(series_h, series)
    ld_ew = [
        load(ew_h.at[:, pl.ds(pl.multiple_of(zz * 128, 128), 128)], ew.at[k])
        for k, zz in enumerate(z_order)
    ]
    barrier = pltpu.get_barrier_semaphore()
    greeted = head_devs + sum_devs[:2] + sum_devs[3:] + [y_to[off] for off in range(1, NY)] + kv_devs
    for dev in greeted:
        pl.semaphore_signal(barrier, inc=1, device_id=dev, device_id_type=MESH)
    ld_ow = load(ow_h, ow)
    ld_vec = [load(r, vec.at[i]) for i, r in enumerate((eb_h, n1g_h, n1b_h, n2g_h, n2b_h))]
    ld_qkv = [load(a, b) for a, b in ((qw_h, qw), (kw_h, kw), (vw_h, vw))]
    ld_ffn = [load(a, b) for a, b in ((fi_h, fi), (fo_h, fo))]

    ld_series.wait()
    s_stack = stacked(series[...])

    def emb_step(k):
        ld_ew[k].wait()
        r = mxu(s_stack, side_by_side(ew[k]))
        epart[k] = quads(r, ROWS, 128).T.reshape(NC, DH, ROWS)

    emb_step(0)
    ld_ow.wait()
    pl.semaphore_wait(barrier, len(greeted))

    core_cps = [send(epart.at[0, oc], cbuf.at[0], core_dev)]
    fence()
    emb_step(1)
    core_cps.append(send(epart.at[1, oc], cbuf.at[1], core_dev))
    fence()
    z_cps = []

    def to_chip(k):
        core_cps[k].wait_recv()
        sbuf[k] = epart[k, c] + cbuf[k]
        z_cps.append(send(sbuf.at[k], rsbuf.at[k], sum_devs[k]))

    to_chip(0)
    emb_step(2)
    core_cps.append(send(epart.at[2, oc], cbuf.at[2], core_dev))
    fence()
    to_chip(1)
    emb_step(3)
    core_cps.append(send(epart.at[3, oc], cbuf.at[3], core_dev))
    fence()
    to_chip(2)
    to_chip(3)

    xrows = pl.ds(pl.multiple_of(x * 16, 16), 16)
    gath[c, x, zh] = ow[xrows, :]
    w_z = [send(gath.at[c, x, zh], gath.at[c, x, zh], dev) for dev in z_devs]
    fence()

    for ld in ld_vec + ld_qkv:
        ld.wait()
    kt = kw[...]
    wqkv[...] = stacked(jnp.concatenate([qw[...], vw[...], kt, kt], axis=0))
    for i, j in enumerate((0, 3, 4)):
        own_vec[i] = column(vec[j, pl.ds(zh, 1), :]).reshape(NC, DH, ROWS)

    for cp in z_cps:
        cp.wait_recv()
    efull[h] = (rsbuf[0] + rsbuf[1]) + (rsbuf[2] + rsbuf[3]) + own_vec[0, c]

    def gather_heads(buf, meanwhile):
        zs = [send(buf.at[h], buf.at[h], dev) for dev in z_devs]
        cs = [send(buf.at[h], buf.at[h], core_dev)]
        fence()
        meanwhile()
        for k in (1, 2, 0):
            zs[k].wait_recv()
            hs = ((zh + NZH - Z_OFFS[k]) % NZH) * NC + c
            cs.append(send(buf.at[hs], buf.at[hs], core_dev))
        for cp in cs:
            cp.wait_recv()

    w_x = []

    def prepare_ffn_in():
        for cp in w_z:
            cp.wait_recv()
        w_x.extend(send(gath.at[c, x], gath.at[c, x], dev) for dev in x_devs)
        ld_ffn[0].wait()
        fit[...] = stacked(fi[...].T)

    gather_heads(efull, prepare_ffn_in)

    emb_t = efull[...].reshape(D, ROWS)
    qkv = quads(mxu(wqkv[...], side_by_side(emb_t)), 4 * DH, ROWS)
    qsend[...] = qkv[:DH] * (math.log2(math.e) / math.sqrt(DH))
    kk = qkv[2 * DH :].T
    left = lax.broadcasted_iota(jnp.int32, (DH, 128), 1) < DH
    kvsend[0] = jnp.where(left, kk[:DH], kk[DH:])
    kvsend[1] = qkv[DH : 2 * DH]

    q_cps, kv_cps = {}, {}

    def send_kv(*slots):
        for i in slots:
            kv_cps[i] = send(kvsend, kvbuf.at[i - 1], kv_devs[i - 1])

    def send_q(*slots):
        for off in slots:
            q_cps[off] = send(qsend, qbuf.at[off], y_to[off])

    for i, off in zip(KV_SENDS, Q_SENDS):
        send_kv(i)
        send_q(off)
    fence()

    for cp in w_x:
        cp.wait_recv()
    w_c = send(gath.at[c], gath.at[c], core_dev)
    ld_ffn[1].wait()
    for z in range(NZH):
        fot[z] = stacked(fo[:, z * 128 : (z + 1) * 128].T)
        n1g[pl.ds(z * 128, 128), :] = column(vec[1, z : z + 1, :])
        n1b[pl.ds(z * 128, 128), :] = column(vec[2, z : z + 1, :])
    def put_key(i, pack):
        other = pltpu.roll(pack, DH, 1)
        for j, kd in enumerate((jnp.where(left, pack, other), jnp.where(left, other, pack))):
            top, rest = halves(kd)
            rows = slice(i * ROWS + j * DH, i * ROWS + (j + 1) * DH)
            kst[rows, :128] = top
            kst[rows, 128:] = rest

    def put_query(j, qt):
        top, rest = halves(qt)
        cols = slice(j * ROWS, (j + 1) * ROWS)
        for r in range(2):
            qst[2 * r * DH : (2 * r + 1) * DH, cols] = top
            qst[(2 * r + 1) * DH : (2 * r + 2) * DH, cols] = rest

    def put_value(i, vt):
        vst[:, i * ROWS : (i + 1) * ROWS] = stacked(vt)

    def put_kv(i):
        kv = kvbuf.at[i - 1] if i else kvsend
        put_key(i, kv[0])
        put_value(i, kv[1])

    put_kv(0)
    put_query(0, qsend[...])
    places = {off: 2 * pair + j for pair in range(4) for j, off in enumerate(Q_PAIRS[pair])}
    for i, off in zip(KV_SENDS, Q_SENDS):
        kv_cps[i].wait_recv()
        put_kv(i)
        q_cps[off].wait_recv()
        put_query(places[off], qbuf[off])

    o_cps = {}
    for pair in (3, 2, 1, 0):
        s = mxu(kst[...], qst[:, 2 * pair * ROWS : (2 * pair + 2) * ROWS])
        top_score = jnp.max(s, axis=0, keepdims=True)
        p = jnp.exp2(s - top_score)
        total = jnp.sum(p, axis=0, keepdims=True)
        p_top, p_rest = halves(p)
        o = mxu(vst[...], p_top) + mxu(vst[...], p_rest)
        o = o[:DH] + o[DH:]
        for j in (1, 0):
            off = Q_PAIRS[pair][j]
            cols = slice(j * ROWS, (j + 1) * ROWS)
            osend[off, :DH] = o[:, cols]
            osend[off, DH : DH + 8] = jnp.concatenate(
                [
                    jnp.broadcast_to(top_score[:, cols], (4, ROWS)),
                    jnp.broadcast_to(total[:, cols], (4, ROWS)),
                ],
                axis=0,
            )
            if off:
                o_cps[off] = send(osend.at[off], obuf.at[off], y_from[off])
        if pair:
            fence()

    w_c.wait_recv()
    for z in range(NZH):
        block = jnp.concatenate(
            [gath[par, xx, z] for par in range(NC) for xx in range(NX)], axis=0
        )
        top, rest = halves(block.T)
        wot[:D, z * 128 : (z + 1) * 128] = top
        wot[D:, z * 128 : (z + 1) * 128] = rest


    for off in range(1, NY):
        o_cps[off].wait_recv()
    tops = [osend[0, DH : DH + 1]] + [obuf[off, DH : DH + 1] for off in range(1, NY)]
    best = functools.reduce(jnp.maximum, tops)
    scales = [jnp.exp2(t - best) for t in tops]
    denom = scales[0] * osend[0, DH + 4 : DH + 5]
    acc = scales[0] * osend[0, :DH]
    for off in range(1, NY):
        denom += scales[off] * obuf[off, DH + 4 : DH + 5]
        acc += scales[off] * obuf[off, :DH]
    mfull[h] = acc / denom

    gather_heads(mfull, lambda: None)

    mixed_t = mfull[...].reshape(D, ROWS)
    resid = emb_t + quads(mxu(wot[...], side_by_side(mixed_t)), D, ROWS)
    centre = jnp.sum(resid, axis=0, keepdims=True) * (1.0 / D)
    spread = resid - centre
    variance = jnp.sum(spread * spread, axis=0, keepdims=True) * (1.0 / D)
    normed = spread * lax.rsqrt(variance + EPS) * n1g[...] + n1b[...]
    normed_ref[...] = normed.reshape(NHEAD, DH, ROWS)
    hid = quads(mxu(fit[...], side_by_side(normed)), FF_PART, ROWS)
    hid = hid * (1.0 + lax.erf(hid * (1.0 / math.sqrt(2.0)))) * 0.5
    hid2 = side_by_side(hid)

    fcore = []
    for k in range(4):
        fpart[k] = quads(mxu(fot[z_order[k]], hid2), 128, ROWS).reshape(NC, DH, ROWS)
        fcore.append(send(fpart.at[k, oc], fcbuf.at[k], core_dev))
        fence()
    fz = []
    for k in range(4):
        fcore[k].wait_recv()
        chip_sum = fpart[k, c] + fcbuf[k]
        fsbuf[k] = chip_sum + normed_ref[h] if k == 2 else chip_sum
        fz.append(send(fsbuf.at[k], frsbuf.at[k], sum_devs[k]))
    for cp in fz:
        cp.wait_recv()
    r2 = (frsbuf[0] + frsbuf[1]) + (frsbuf[2] + frsbuf[3])

    mean_own = jnp.sum(r2, axis=0, keepdims=True) * (1.0 / DH)
    dev_own = r2 - mean_own
    m2_own = jnp.sum(dev_own * dev_own, axis=0, keepdims=True)
    stat[...] = jnp.concatenate(
        [jnp.broadcast_to(mean_own, (4, ROWS)), jnp.broadcast_to(m2_own, (4, ROWS))], axis=0
    )
    st = [send(stat, statbuf.at[i], dev) for i, dev in enumerate(head_devs)]
    for cp in st:
        cp.wait_recv()
    means = [mean_own] + [statbuf[i, 0:1] for i in range(7)]
    mean = functools.reduce(jnp.add, means) * (1.0 / NHEAD)
    m2 = functools.reduce(jnp.add, [m2_own] + [statbuf[i, 4:5] for i in range(7)])
    m2 += DH * functools.reduce(jnp.add, [(m - mean) * (m - mean) for m in means])
    scale = lax.rsqrt(m2 * (1.0 / D) + EPS)
    out_ref[...] = (r2 - mean) * scale * own_vec[1, c] + own_vec[2, c]
    drain()


def on_device(series, emb_weight, emb_bias, q_weight, k_weight, v_weight, out_weight,
              norm1_gain, norm1_bias, ffn_in, ffn_out, norm2_gain, norm2_bias):
    vec4 = lambda a: a.reshape(4, 128)
    vm = lambda *shape: pltpu.VMEM(shape, F32)
    vb = lambda *shape: pltpu.VMEM(shape, BF16)
    block = (DH, ROWS)
    scratch = [
        vm(ROWS, 1024), vm(4, 1024, 128), vm(DH, D), vm(DH, D), vm(DH, D), vm(DH, D),
        vm(D, FF_PART), vm(FF_PART, D), vm(5, 4, 128),
        vb(8 * DH, D), vb(2 * FF_PART, D), vb(4, 256, FF_PART), vb(2 * D, D),
        vm(NC, NX, NZH, 16, D), vm(D, ROWS), vm(D, ROWS), vm(3, NC, *block),
        vm(4, NC, *block), vm(4, *block), vm(4, *block), vm(4, *block), vm(NHEAD, *block),
        vm(*block), vm(2, *block), vm(NY, *block), vm(7, 2, *block),
        vb(1024, 256), vb(256, 1024), vb(128, 1024),
        vm(NY, DH + 8, ROWS), vm(NY, DH + 8, ROWS), vm(NHEAD, *block), vm(NHEAD, *block),
        vm(4, NC, *block), vm(4, *block), vm(4, *block), vm(4, *block),
        vm(8, ROWS), vm(7, 8, ROWS),
        pltpu.SemaphoreType.DMA((16,)), pltpu.SemaphoreType.DMA((COPIES,)),
        pltpu.SemaphoreType.DMA((COPIES,)), pltpu.SemaphoreType.REGULAR,
    ]
    return pl.pallas_call(
        layer_kernel,
        out_shape=jax.ShapeDtypeStruct(block, F32),
        in_specs=[pl.BlockSpec(memory_space=pl.ANY)] * 13,
        out_specs=pl.BlockSpec(memory_space=pltpu.VMEM),
        scratch_shapes=scratch,
        compiler_params=pltpu.CompilerParams(
            collective_id=0, has_side_effects=True, vmem_limit_bytes=60 * 1024 * 1024
        ),
        name="layer",
    )(series, emb_weight, vec4(emb_bias), q_weight.T, k_weight.T, v_weight.T, out_weight,
      vec4(norm1_gain), vec4(norm1_bias), ffn_in, ffn_out, vec4(norm2_gain), vec4(norm2_bias))


def solution(mesh):
    return jax.shard_map(
        on_device,
        mesh=mesh,
        in_specs=(
            P("var", "head"), P("head", None), P(), P(None, "head"), P(None, "head"),
            P(None, "head"), P("head", None), P(), P(), P(None, "head"), P("head", None), P(), P(),
        ),
        out_specs=P("head", "var"),
        check_vma=False,
    )
```

```python
import functools
import math

import jax
import jax.numpy as jnp
from jax import lax
from jax.experimental import pallas as pl
from jax.experimental.pallas import tpu as pltpu
from jax.sharding import PartitionSpec as P

MESH = pl.DeviceIdType.MESH
F32 = jnp.float32
BF16 = jnp.bfloat16

D = 512
FF_PART = 256
DH = 64
ROWS = 128
NY, NX, NZL, NZH, NC = 8, 4, 2, 4, 2
NHEAD = NZH * NC
Z_OFFS = (2, 1, 3)
Q_PAIRS = ((0, 1), (7, 2), (6, 3), (5, 4))
KV_OFFS = ((1, 0), (3, 0), (0, 1), (1, 1), (3, 1), (2, 0), (2, 1))
KV_SENDS = (7, 6, 4, 5, 3, 1, 2)
Q_SENDS = (4, 3, 5, 2, 6, 7, 1)
COPIES = 96
EPS = 1e-05


def halves(x):
    top = x.astype(BF16)
    return top, (x - top.astype(F32)).astype(BF16)


def mxu(a, b):
    return lax.dot_general(a, b, (((1,), (0,)), ((), ())), preferred_element_type=F32)


def quads(r, m, n):
    return r[:m, :n] + ((r[:m, n:] + r[m:, :n]) + r[m:, n:])


def side_by_side(x):
    return jnp.concatenate(halves(x), axis=1)


def stacked(x):
    return jnp.concatenate(halves(x), axis=0)


def column(row):
    return jnp.broadcast_to(row, (128, 128)).T


def layer_kernel(
    series_h, ew_h, eb_h, qw_h, kw_h, vw_h, ow_h, n1g_h, n1b_h, fi_h, fo_h, n2g_h, n2b_h,
    out_ref,
    series, ew, qw, kw, vw, ow, fi, fo, vec,
    wqkv, fit, fot, wot, gath, n1g, n1b, own_vec,
    epart, cbuf, sbuf, rsbuf, efull,
    qsend, kvsend, qbuf, kvbuf, kst, qst, vst,
    osend, obuf, mfull, normed_ref,
    fpart, fcbuf, fsbuf, frsbuf, stat, statbuf,
    lsem, ssem, rsem, own_sem,
):
    v = lax.axis_index("var")
    h = lax.axis_index("head")
    y, x, zl = v // (NX * NZL), (v // NZL) % NX, v % NZL
    zh, c = h // NC, h % NC
    oc = 1 - c

    def at(y_, x_, zl_, zh_, c_):
        return ((y_ * NX + x_) * NZL + zl_, zh_ * NC + c_)

    core_dev = at(y, x, zl, zh, oc)
    z_devs = [at(y, x, zl, (zh + off) % NZH, c) for off in Z_OFFS]
    sum_offs = (2, 1 + 2 * zl, 0, 3 - 2 * zl)
    z_order = [(zh + off) % NZH for off in sum_offs]
    sum_devs = [at(y, x, 1 - zl, zz, c) for zz in z_order]
    x_devs = [at(y, (x + off) % NX, zl, zh, c) for off in (2, 1, 3)]
    y_to = {off: at((y + off) % NY, x, zl, zh, c) for off in range(1, NY)}
    y_from = {off: at((y + NY - off) % NY, x, zl, zh, c) for off in range(1, NY)}
    kv_devs = [at(y, (x + dx) % NX, (zl + dz) % NZL, zh, c) for dx, dz in KV_OFFS]

    count = [0]
    pending = []

    def send(src, dst, dev):
        i = count[0]
        count[0] += 1
        cp = pltpu.make_async_remote_copy(
            src_ref=src, dst_ref=dst, send_sem=ssem.at[i], recv_sem=rsem.at[i],
            device_id=dev, device_id_type=MESH,
        )
        cp.start()
        pending.append(cp)
        return cp

    def drain(keep=0):
        while len(pending) > keep:
            pending.pop(0).wait_send()

    def fence():
        pl.semaphore_signal(own_sem, 1)
        pl.semaphore_wait(own_sem, 1)

    lcount = [0]

    def load(src, dst):
        i = lcount[0]
        lcount[0] += 1
        cp = pltpu.make_async_copy(src, dst, lsem.at[i])
        cp.start()
        return cp

    ld_series = load(series_h, series)

    def load_ew(k):
        cols = pl.ds(pl.multiple_of(z_order[k] * 128, 128), 128)
        return load(ew_h.at[:, cols], ew.at[k])

    ld_ew = [load_ew(0)]
    barrier = pltpu.get_barrier_semaphore()
    greeted = z_devs + [core_dev] + sum_devs[:2] + sum_devs[3:] + [y_to[off] for off in range(1, NY)] + kv_devs
    for dev in greeted:
        pl.semaphore_signal(barrier, inc=1, device_id=dev, device_id_type=MESH)
    ld_ew += [load_ew(k) for k in (1, 2, 3)]

    ld_series.wait()
    s_stack = stacked(series[...])

    def emb_step(k):
        ld_ew[k].wait()
        r = mxu(s_stack, side_by_side(ew[k]))
        epart[k] = quads(r, ROWS, 128).T.reshape(NC, DH, ROWS)

    emb_step(0)
    ld_ow = load(ow_h, ow)
    ld_vec = [load(r, vec.at[i]) for i, r in enumerate((eb_h, n1g_h, n1b_h, n2g_h, n2b_h))]
    ld_qkv = [load(a, b) for a, b in ((qw_h, qw), (kw_h, kw), (vw_h, vw))]
    ld_ffn = [load(a, b) for a, b in ((fi_h, fi), (fo_h, fo))]
    pl.semaphore_wait(barrier, len(greeted))

    core_cps = [send(epart.at[0, oc], cbuf.at[0], core_dev)]
    fence()
    emb_step(1)
    core_cps.append(send(epart.at[1, oc], cbuf.at[1], core_dev))
    fence()
    z_cps = []

    def to_chip(k):
        core_cps[k].wait_recv()
        sbuf[k] = epart[k, c] + cbuf[k]
        z_cps.append(send(sbuf.at[k], rsbuf.at[k], sum_devs[k]))

    to_chip(0)
    emb_step(2)
    core_cps.append(send(epart.at[2, oc], cbuf.at[2], core_dev))
    fence()
    to_chip(1)
    emb_step(3)
    core_cps.append(send(epart.at[3, oc], cbuf.at[3], core_dev))
    fence()
    to_chip(2)
    to_chip(3)

    ld_ow.wait()
    xrows = pl.ds(pl.multiple_of(x * 16, 16), 16)
    gath[c, x, zh] = ow[xrows, :]
    w_z = [send(gath.at[c, x, zh], gath.at[c, x, zh], dev) for dev in z_devs]
    fence()

    for ld in ld_vec + ld_qkv:
        ld.wait()
    kt = kw[...]
    wqkv[...] = stacked(jnp.concatenate([qw[...], vw[...], kt, kt], axis=0))
    for i, j in enumerate((0, 3, 4)):
        own_vec[i] = column(vec[j, pl.ds(zh, 1), :]).reshape(NC, DH, ROWS)

    for cp in z_cps:
        cp.wait_recv()
    efull[h] = (rsbuf[0] + rsbuf[1]) + (rsbuf[2] + rsbuf[3]) + own_vec[0, c]

    def gather_heads(buf, meanwhile):
        zs = [send(buf.at[h], buf.at[h], dev) for dev in z_devs]
        cs = [send(buf.at[h], buf.at[h], core_dev)]
        fence()
        drain(keep=4)
        meanwhile()
        for k in (1, 2, 0):
            zs[k].wait_recv()
            hs = ((zh + NZH - Z_OFFS[k]) % NZH) * NC + c
            cs.append(send(buf.at[hs], buf.at[hs], core_dev))
        for cp in cs:
            cp.wait_recv()

    def prepare_ffn_in():
        for cp in w_z:
            cp.wait_recv()
        ld_ffn[0].wait()
        fit[...] = stacked(fi[...].T)

    gather_heads(efull, prepare_ffn_in)

    emb_t = efull[...].reshape(D, ROWS)
    qkv = quads(mxu(wqkv[...], side_by_side(emb_t)), 4 * DH, ROWS)
    qsend[...] = qkv[:DH] * (math.log2(math.e) / math.sqrt(DH))
    kk = qkv[2 * DH :].T
    left = lax.broadcasted_iota(jnp.int32, (DH, 128), 1) < DH
    kvsend[0] = jnp.where(left, kk[:DH], kk[DH:])
    kvsend[1] = qkv[DH : 2 * DH]

    q_cps, kv_cps = {}, {}

    def send_kv(*slots):
        for i in slots:
            kv_cps[i] = send(kvsend, kvbuf.at[i - 1], kv_devs[i - 1])

    def send_q(*slots):
        for off in slots:
            q_cps[off] = send(qsend, qbuf.at[off], y_to[off])

    for i, off in zip(KV_SENDS, Q_SENDS):
        send_kv(i)
        send_q(off)
    fence()
    drain(keep=14)

    ld_ffn[1].wait()
    for z in range(NZH):
        fot[z] = stacked(fo[:, z * 128 : (z + 1) * 128].T)
        n1g[pl.ds(z * 128, 128), :] = column(vec[1, z : z + 1, :])
        n1b[pl.ds(z * 128, 128), :] = column(vec[2, z : z + 1, :])
    def put_key(i, pack):
        other = pltpu.roll(pack, DH, 1)
        for j, kd in enumerate((jnp.where(left, pack, other), jnp.where(left, other, pack))):
            top, rest = halves(kd)
            rows = slice(i * ROWS + j * DH, i * ROWS + (j + 1) * DH)
            kst[rows, :128] = top
            kst[rows, 128:] = rest

    def put_query(j, qt):
        top, rest = halves(qt)
        cols = slice(j * ROWS, (j + 1) * ROWS)
        for r in range(2):
            qst[2 * r * DH : (2 * r + 1) * DH, cols] = top
            qst[(2 * r + 1) * DH : (2 * r + 2) * DH, cols] = rest

    def put_value(i, vt):
        vst[:, i * ROWS : (i + 1) * ROWS] = stacked(vt)

    def put_kv(i):
        kv = kvbuf.at[i - 1] if i else kvsend
        put_key(i, kv[0])
        put_value(i, kv[1])

    put_kv(0)
    put_query(0, qsend[...])
    places = {off: 2 * pair + j for pair in range(4) for j, off in enumerate(Q_PAIRS[pair])}
    for i, off in zip(KV_SENDS, Q_SENDS):
        kv_cps[i].wait_recv()
        put_kv(i)
        q_cps[off].wait_recv()
        put_query(places[off], qbuf[off])

    o_cps = {}
    for pair in (3, 2, 1, 0):
        s = mxu(kst[...], qst[:, 2 * pair * ROWS : (2 * pair + 2) * ROWS])
        top_score = jnp.max(s, axis=0, keepdims=True)
        p = jnp.exp2(s - top_score)
        total = jnp.sum(p, axis=0, keepdims=True)
        p_top, p_rest = halves(p)
        o = mxu(vst[...], p_top) + mxu(vst[...], p_rest)
        o = o[:DH] + o[DH:]
        for j in (1, 0):
            off = Q_PAIRS[pair][j]
            cols = slice(j * ROWS, (j + 1) * ROWS)
            osend[off, :DH] = o[:, cols]
            osend[off, DH : DH + 1] = top_score[:, cols]
            osend[off, DH + 1 : DH + 2] = total[:, cols]
            if off:
                o_cps[off] = send(osend.at[off], obuf.at[off], y_from[off])
        if pair:
            fence()

    w_x = [send(gath.at[c, x], gath.at[c, x], dev) for dev in x_devs]
    drain(keep=10)

    def prepare_out_weight():
        for cp in w_x:
            cp.wait_recv()
        send(gath.at[c], gath.at[c], core_dev).wait_recv()
        for z in range(NZH):
            block = jnp.concatenate(
                [gath[par, xx, z] for par in range(NC) for xx in range(NX)], axis=0
            )
            top, rest = halves(block.T)
            wot[:D, z * 128 : (z + 1) * 128] = top
            wot[D:, z * 128 : (z + 1) * 128] = rest

    for off in range(1, NY):
        o_cps[off].wait_recv()
    tops = [osend[0, DH : DH + 1]] + [obuf[off, DH : DH + 1] for off in range(1, NY)]
    best = functools.reduce(jnp.maximum, tops)
    scales = [jnp.exp2(t - best) for t in tops]
    denom = scales[0] * osend[0, DH + 1 : DH + 2]
    acc = scales[0] * osend[0, :DH]
    for off in range(1, NY):
        denom += scales[off] * obuf[off, DH + 1 : DH + 2]
        acc += scales[off] * obuf[off, :DH]
    mfull[h] = acc / denom

    gather_heads(mfull, prepare_out_weight)

    mixed_t = mfull[...].reshape(D, ROWS)
    resid = emb_t + quads(mxu(wot[...], side_by_side(mixed_t)), D, ROWS)
    centre = jnp.sum(resid, axis=0, keepdims=True) * (1.0 / D)
    spread = resid - centre
    variance = jnp.sum(spread * spread, axis=0, keepdims=True) * (1.0 / D)
    normed = spread * lax.rsqrt(variance + EPS) * n1g[...] + n1b[...]
    normed_ref[...] = normed.reshape(NHEAD, DH, ROWS)
    hid = quads(mxu(fit[...], side_by_side(normed)), FF_PART, ROWS)
    hid = hid * (1.0 + lax.erf(hid * (1.0 / math.sqrt(2.0)))) * 0.5
    hid2 = side_by_side(hid)

    fcore = []
    for k in range(4):
        fpart[k] = quads(mxu(fot[z_order[k]], hid2), 128, ROWS).reshape(NC, DH, ROWS)
        fcore.append(send(fpart.at[k, oc], fcbuf.at[k], core_dev))
        fence()
    fz = []
    for k in range(4):
        fcore[k].wait_recv()
        chip_sum = fpart[k, c] + fcbuf[k]
        fsbuf[k] = chip_sum + normed_ref[h] if k == 2 else chip_sum
        fz.append(send(fsbuf.at[k], frsbuf.at[k], sum_devs[k]))
    drain(keep=8)
    for cp in fz:
        cp.wait_recv()
    r2 = (frsbuf[0] + frsbuf[1]) + (frsbuf[2] + frsbuf[3])

    mean_own = jnp.sum(r2, axis=0, keepdims=True) * (1.0 / DH)
    dev_own = r2 - mean_own
    m2_own = jnp.sum(dev_own * dev_own, axis=0, keepdims=True)
    stat[0, 0:1] = mean_own
    stat[0, 1:2] = m2_own
    send(stat.at[0], statbuf.at[3], core_dev).wait_recv()
    gap = mean_own - statbuf[3, 0:1]
    mean_pair = 0.5 * (mean_own + statbuf[3, 0:1])
    m2_pair = m2_own + statbuf[3, 1:2] + (0.5 * DH) * gap * gap
    stat[1, 0:1] = mean_pair
    stat[1, 1:2] = m2_pair
    st = [send(stat.at[1], statbuf.at[i], dev) for i, dev in enumerate(z_devs)]
    drain(keep=3)
    for cp in st:
        cp.wait_recv()
    means = [mean_pair] + [statbuf[i, 0:1] for i in range(3)]
    mean = functools.reduce(jnp.add, means) * (1.0 / NZH)
    m2 = functools.reduce(jnp.add, [m2_pair] + [statbuf[i, 1:2] for i in range(3)])
    m2 += 2 * DH * functools.reduce(jnp.add, [(m - mean) * (m - mean) for m in means])
    scale = lax.rsqrt(m2 * (1.0 / D) + EPS)
    out_ref[...] = (r2 - mean) * scale * own_vec[1, c] + own_vec[2, c]
    drain()


def on_device(series, emb_weight, emb_bias, q_weight, k_weight, v_weight, out_weight,
              norm1_gain, norm1_bias, ffn_in, ffn_out, norm2_gain, norm2_bias):
    vec4 = lambda a: a.reshape(4, 128)
    vm = lambda *shape: pltpu.VMEM(shape, F32)
    vb = lambda *shape: pltpu.VMEM(shape, BF16)
    block = (DH, ROWS)
    scratch = [
        vm(ROWS, 1024), vm(4, 1024, 128), vm(DH, D), vm(DH, D), vm(DH, D), vm(DH, D),
        vm(D, FF_PART), vm(FF_PART, D), vm(5, 4, 128),
        vb(8 * DH, D), vb(2 * FF_PART, D), vb(4, 256, FF_PART), vb(2 * D, D),
        vm(NC, NX, NZH, 16, D), vm(D, ROWS), vm(D, ROWS), vm(3, NC, *block),
        vm(4, NC, *block), vm(4, *block), vm(4, *block), vm(4, *block), vm(NHEAD, *block),
        vm(*block), vm(2, *block), vm(NY, *block), vm(7, 2, *block),
        vb(1024, 256), vb(256, 1024), vb(128, 1024),
        vm(NY, DH + 2, ROWS), vm(NY, DH + 2, ROWS), vm(NHEAD, *block), vm(NHEAD, *block),
        vm(4, NC, *block), vm(4, *block), vm(4, *block), vm(4, *block),
        vm(2, 2, ROWS), vm(4, 2, ROWS),
        pltpu.SemaphoreType.DMA((16,)), pltpu.SemaphoreType.DMA((COPIES,)),
        pltpu.SemaphoreType.DMA((COPIES,)), pltpu.SemaphoreType.REGULAR,
    ]
    return pl.pallas_call(
        layer_kernel,
        out_shape=jax.ShapeDtypeStruct(block, F32),
        in_specs=[pl.BlockSpec(memory_space=pl.ANY)] * 13,
        out_specs=pl.BlockSpec(memory_space=pltpu.VMEM),
        scratch_shapes=scratch,
        compiler_params=pltpu.CompilerParams(
            collective_id=0, has_side_effects=True, vmem_limit_bytes=60 * 1024 * 1024
        ),
        name="layer",
    )(series, emb_weight, vec4(emb_bias), q_weight.T, k_weight.T, v_weight.T, out_weight,
      vec4(norm1_gain), vec4(norm1_bias), ffn_in, ffn_out, vec4(norm2_gain), vec4(norm2_bias))


def solution(mesh):
    return jax.shard_map(
        on_device,
        mesh=mesh,
        in_specs=(
            P("var", "head"), P("head", None), P(), P(None, "head"), P(None, "head"),
            P(None, "head"), P("head", None), P(), P(), P(None, "head"), P("head", None), P(), P(),
        ),
        out_specs=P("head", "var"),
        check_vma=False,
    )
```

```python
import functools
import math

import jax
import jax.numpy as jnp
from jax import lax
from jax.experimental import pallas as pl
from jax.experimental.pallas import tpu as pltpu
from jax.sharding import PartitionSpec as P

MESH = pl.DeviceIdType.MESH
F32 = jnp.float32
BF16 = jnp.bfloat16

D = 512
FF_PART = 256
DH = 64
ROWS = 128
NY, NX, NZL, NZH, NC = 8, 4, 2, 4, 2
NHEAD = NZH * NC
Z_OFFS = (2, 1, 3)
Q_PAIRS = ((0, 1), (7, 2), (6, 3), (5, 4))
KV_OFFS = ((1, 0), (3, 0), (0, 1), (1, 1), (3, 1), (2, 0), (2, 1))
KV_SENDS = (7, 6, 4, 5, 3, 1, 2)
Q_SENDS = (4, 3, 5, 2, 6, 7, 1)
COPIES = 96
EPS = 1e-05


def halves(x):
    top = x.astype(BF16)
    return top, (x - top.astype(F32)).astype(BF16)


def mxu(a, b):
    return lax.dot_general(a, b, (((1,), (0,)), ((), ())), preferred_element_type=F32)


def quads(r, m, n):
    return r[:m, :n] + ((r[:m, n:] + r[m:, :n]) + r[m:, n:])


def side_by_side(x):
    return jnp.concatenate(halves(x), axis=1)


def stacked(x):
    return jnp.concatenate(halves(x), axis=0)


def column(row):
    return jnp.broadcast_to(row, (128, 128)).T


def layer_kernel(
    series_h, ew_h, eb_h, qw_h, kw_h, vw_h, ow_h, n1g_h, n1b_h, fi_h, fo_h, n2g_h, n2b_h,
    out_ref,
    series, ew, qw, kw, vw, ow, fi, fo, vec,
    wqkv, fit, fot, wot, gath, n1g, n1b, own_vec,
    epart, cbuf, sbuf, rsbuf, efull,
    qsend, kvsend, qbuf, kvbuf, kst, qst, vst,
    osend, obuf, mfull, normed_ref,
    fpart, fcbuf, fsbuf, frsbuf, stat, statbuf,
    lsem, ssem, rsem, own_sem,
):
    v = lax.axis_index("var")
    h = lax.axis_index("head")
    y, x, zl = v // (NX * NZL), (v // NZL) % NX, v % NZL
    zh, c = h // NC, h % NC
    oc = 1 - c

    def at(y_, x_, zl_, zh_, c_):
        return ((y_ * NX + x_) * NZL + zl_, zh_ * NC + c_)

    core_dev = at(y, x, zl, zh, oc)
    z_devs = [at(y, x, zl, (zh + off) % NZH, c) for off in Z_OFFS]
    sum_offs = (2, 1 + 2 * zl, 0, 3 - 2 * zl)
    z_order = [(zh + off) % NZH for off in sum_offs]
    sum_devs = [at(y, x, 1 - zl, zz, c) for zz in z_order]
    x_devs = [at(y, (x + off) % NX, zl, zh, c) for off in (2, 1, 3)]
    y_to = {off: at((y + off) % NY, x, zl, zh, c) for off in range(1, NY)}
    y_from = {off: at((y + NY - off) % NY, x, zl, zh, c) for off in range(1, NY)}
    kv_devs = [at(y, (x + dx) % NX, (zl + dz) % NZL, zh, c) for dx, dz in KV_OFFS]

    count = [0]
    pending = []

    def send(src, dst, dev):
        i = count[0]
        count[0] += 1
        cp = pltpu.make_async_remote_copy(
            src_ref=src, dst_ref=dst, send_sem=ssem.at[i], recv_sem=rsem.at[i],
            device_id=dev, device_id_type=MESH,
        )
        cp.start()
        pending.append(cp)
        return cp

    def drain(keep=0):
        while len(pending) > keep:
            pending.pop(0).wait_send()

    def fence():
        pl.semaphore_signal(own_sem, 1)
        pl.semaphore_wait(own_sem, 1)

    lcount = [0]

    def load(src, dst):
        i = lcount[0]
        lcount[0] += 1
        cp = pltpu.make_async_copy(src, dst, lsem.at[i])
        cp.start()
        return cp

    ld_series = load(series_h, series)

    def load_ew(k):
        cols = pl.ds(pl.multiple_of(z_order[k] * 128, 128), 128)
        return load(ew_h.at[:, cols], ew.at[k])

    ld_ew = [load_ew(0)]
    barrier = pltpu.get_barrier_semaphore()
    greeted = z_devs + [core_dev] + sum_devs[:2] + sum_devs[3:] + [y_to[off] for off in range(1, NY)] + kv_devs
    for dev in greeted:
        pl.semaphore_signal(barrier, inc=1, device_id=dev, device_id_type=MESH)
    ld_ew += [load_ew(k) for k in (1, 2, 3)]

    ld_series.wait()
    s_stack = stacked(series[...])

    def emb_step(k):
        ld_ew[k].wait()
        r = mxu(s_stack, side_by_side(ew[k]))
        epart[k] = quads(r, ROWS, 128).T.reshape(NC, DH, ROWS)

    emb_step(0)
    ld_ow = load(ow_h, ow)
    ld_vec = [load(r, vec.at[i]) for i, r in enumerate((eb_h, n1g_h, n1b_h, n2g_h, n2b_h))]
    ld_qkv = [load(a, b) for a, b in ((qw_h, qw), (kw_h, kw), (vw_h, vw))]
    ld_ffn = [load(a, b) for a, b in ((fi_h, fi), (fo_h, fo))]
    pl.semaphore_wait(barrier, len(greeted))

    core_cps = [send(epart.at[0, oc], cbuf.at[0], core_dev)]
    fence()
    emb_step(1)
    core_cps.append(send(epart.at[1, oc], cbuf.at[1], core_dev))
    fence()
    z_cps = []

    def to_chip(k):
        core_cps[k].wait_recv()
        sbuf[k] = epart[k, c] + cbuf[k]
        z_cps.append(send(sbuf.at[k], rsbuf.at[k], sum_devs[k]))

    to_chip(0)
    emb_step(2)
    core_cps.append(send(epart.at[2, oc], cbuf.at[2], core_dev))
    fence()
    to_chip(1)
    emb_step(3)
    core_cps.append(send(epart.at[3, oc], cbuf.at[3], core_dev))
    fence()
    to_chip(2)
    to_chip(3)

    ld_ow.wait()
    xrows = pl.ds(pl.multiple_of(x * 16, 16), 16)
    gath[c, x, zh] = ow[xrows, :]
    w_z = [send(gath.at[c, x, zh], gath.at[c, x, zh], dev) for dev in z_devs]
    fence()

    for ld in ld_vec + ld_qkv:
        ld.wait()
    kt = kw[...]
    wqkv[...] = stacked(jnp.concatenate([qw[...], vw[...], kt, kt], axis=0))
    for i, j in enumerate((0, 3, 4)):
        own_vec[i] = column(vec[j, pl.ds(zh, 1), :]).reshape(NC, DH, ROWS)

    for cp in z_cps:
        cp.wait_recv()
    efull[h] = (rsbuf[0] + rsbuf[1]) + (rsbuf[2] + rsbuf[3]) + own_vec[0, c]

    def gather_heads(buf, meanwhile):
        zs = [send(buf.at[h], buf.at[h], dev) for dev in z_devs]
        cs = [send(buf.at[h], buf.at[h], core_dev)]
        fence()
        drain(keep=4)
        meanwhile()
        for k in (1, 2, 0):
            zs[k].wait_recv()
            hs = ((zh + NZH - Z_OFFS[k]) % NZH) * NC + c
            cs.append(send(buf.at[hs], buf.at[hs], core_dev))
        for cp in cs:
            cp.wait_recv()

    def prepare_ffn_in():
        for cp in w_z:
            cp.wait_recv()
        ld_ffn[0].wait()
        fit[...] = stacked(fi[...].T)

    gather_heads(efull, prepare_ffn_in)

    emb_t = efull[...].reshape(D, ROWS)
    qkv = quads(mxu(wqkv[...], side_by_side(emb_t)), 4 * DH, ROWS)
    qsend[...] = qkv[:DH] * (math.log2(math.e) / math.sqrt(DH))
    kk = qkv[2 * DH :].T
    left = lax.broadcasted_iota(jnp.int32, (DH, 128), 1) < DH
    kvsend[0] = jnp.where(left, kk[:DH], kk[DH:])
    kvsend[1] = qkv[DH : 2 * DH]

    q_cps, kv_cps = {}, {}

    def send_kv(*slots):
        for i in slots:
            kv_cps[i] = send(kvsend, kvbuf.at[i - 1], kv_devs[i - 1])

    def send_q(*slots):
        for off in slots:
            q_cps[off] = send(qsend, qbuf.at[off], y_to[off])

    for i, off in zip(KV_SENDS, Q_SENDS):
        send_kv(i)
        send_q(off)
    fence()
    drain(keep=14)

    ld_ffn[1].wait()
    for z in range(NZH):
        fot[z] = stacked(fo[:, z * 128 : (z + 1) * 128].T)
        n1g[pl.ds(z * 128, 128), :] = column(vec[1, z : z + 1, :])
        n1b[pl.ds(z * 128, 128), :] = column(vec[2, z : z + 1, :])
    def put_key(i, pack):
        other = pltpu.roll(pack, DH, 1)
        for j, kd in enumerate((jnp.where(left, pack, other), jnp.where(left, other, pack))):
            top, rest = halves(kd)
            rows = slice(i * ROWS + j * DH, i * ROWS + (j + 1) * DH)
            kst[rows, :128] = top
            kst[rows, 128:] = rest

    def put_query(j, qt):
        top, rest = halves(qt)
        cols = slice(j * ROWS, (j + 1) * ROWS)
        for r in range(2):
            qst[2 * r * DH : (2 * r + 1) * DH, cols] = top
            qst[(2 * r + 1) * DH : (2 * r + 2) * DH, cols] = rest

    def put_value(i, vt):
        vst[:, i * ROWS : (i + 1) * ROWS] = stacked(vt)

    def put_kv(i):
        kv = kvbuf.at[i - 1] if i else kvsend
        put_key(i, kv[0])
        put_value(i, kv[1])

    put_kv(0)
    put_query(0, qsend[...])
    places = {off: 2 * pair + j for pair in range(4) for j, off in enumerate(Q_PAIRS[pair])}
    for i, off in zip(KV_SENDS, Q_SENDS):
        kv_cps[i].wait_recv()
        put_kv(i)
        q_cps[off].wait_recv()
        put_query(places[off], qbuf[off])

    o_cps = {}
    for pair in (3, 2, 1, 0):
        s = mxu(kst[...], qst[:, 2 * pair * ROWS : (2 * pair + 2) * ROWS])
        top_score = jnp.max(s, axis=0, keepdims=True)
        p = jnp.exp2(s - top_score)
        total = jnp.sum(p, axis=0, keepdims=True)
        p_top, p_rest = halves(p)
        o = mxu(vst[...], p_top) + mxu(vst[...], p_rest)
        o = o[:DH] + o[DH:]
        for j in (1, 0):
            off = Q_PAIRS[pair][j]
            cols = slice(j * ROWS, (j + 1) * ROWS)
            osend[off, :DH] = o[:, cols]
            osend[off, DH : DH + 1] = top_score[:, cols]
            osend[off, DH + 1 : DH + 2] = total[:, cols]
            if off:
                o_cps[off] = send(osend.at[off], obuf.at[off], y_from[off])
        if pair:
            fence()

    w_x = [send(gath.at[c, x], gath.at[c, x], dev) for dev in x_devs]
    w_c = [send(gath.at[c, x], gath.at[c, x], core_dev)]
    drain(keep=11)

    def prepare_out_weight():
        for k, off in ((1, 1), (2, 3), (0, 2)):
            w_x[k].wait_recv()
            xs = (x + NX - off) % NX
            w_c.append(send(gath.at[c, xs], gath.at[c, xs], core_dev))
        for cp in w_c:
            cp.wait_recv()
        for z in range(NZH):
            block = jnp.concatenate(
                [gath[par, xx, z] for par in range(NC) for xx in range(NX)], axis=0
            )
            top, rest = halves(block.T)
            wot[:D, z * 128 : (z + 1) * 128] = top
            wot[D:, z * 128 : (z + 1) * 128] = rest

    for off in range(1, NY):
        o_cps[off].wait_recv()
    tops = [osend[0, DH : DH + 1]] + [obuf[off, DH : DH + 1] for off in range(1, NY)]
    best = functools.reduce(jnp.maximum, tops)
    scales = [jnp.exp2(t - best) for t in tops]
    denom = scales[0] * osend[0, DH + 1 : DH + 2]
    acc = scales[0] * osend[0, :DH]
    for off in range(1, NY):
        denom += scales[off] * obuf[off, DH + 1 : DH + 2]
        acc += scales[off] * obuf[off, :DH]
    mfull[h] = acc / denom

    gather_heads(mfull, prepare_out_weight)

    mixed_t = mfull[...].reshape(D, ROWS)
    resid = emb_t + quads(mxu(wot[...], side_by_side(mixed_t)), D, ROWS)
    centre = jnp.sum(resid, axis=0, keepdims=True) * (1.0 / D)
    spread = resid - centre
    variance = jnp.sum(spread * spread, axis=0, keepdims=True) * (1.0 / D)
    normed = spread * lax.rsqrt(variance + EPS) * n1g[...] + n1b[...]
    normed_ref[...] = normed.reshape(NHEAD, DH, ROWS)
    hid = quads(mxu(fit[...], side_by_side(normed)), FF_PART, ROWS)
    hid = hid * (1.0 + lax.erf(hid * (1.0 / math.sqrt(2.0)))) * 0.5
    hid2 = side_by_side(hid)

    fcore = []
    for k in range(4):
        fpart[k] = quads(mxu(fot[z_order[k]], hid2), 128, ROWS).reshape(NC, DH, ROWS)
        fcore.append(send(fpart.at[k, oc], fcbuf.at[k], core_dev))
        fence()
    fz = []
    for k in range(4):
        fcore[k].wait_recv()
        chip_sum = fpart[k, c] + fcbuf[k]
        fsbuf[k] = chip_sum + normed_ref[h] if k == 2 else chip_sum
        fz.append(send(fsbuf.at[k], frsbuf.at[k], sum_devs[k]))
    drain(keep=8)
    for cp in fz:
        cp.wait_recv()
    r2 = (frsbuf[0] + frsbuf[1]) + (frsbuf[2] + frsbuf[3])

    mean_own = jnp.sum(r2, axis=0, keepdims=True) * (1.0 / DH)
    dev_own = r2 - mean_own
    m2_own = jnp.sum(dev_own * dev_own, axis=0, keepdims=True)
    stat[0, 0:1] = mean_own
    stat[0, 1:2] = m2_own
    send(stat.at[0], statbuf.at[3], core_dev).wait_recv()
    gap = mean_own - statbuf[3, 0:1]
    mean_pair = 0.5 * (mean_own + statbuf[3, 0:1])
    m2_pair = m2_own + statbuf[3, 1:2] + (0.5 * DH) * gap * gap
    stat[1, 0:1] = mean_pair
    stat[1, 1:2] = m2_pair
    st = [send(stat.at[1], statbuf.at[i], dev) for i, dev in enumerate(z_devs)]
    drain(keep=3)
    for cp in st:
        cp.wait_recv()
    means = [mean_pair] + [statbuf[i, 0:1] for i in range(3)]
    mean = functools.reduce(jnp.add, means) * (1.0 / NZH)
    m2 = functools.reduce(jnp.add, [m2_pair] + [statbuf[i, 1:2] for i in range(3)])
    m2 += 2 * DH * functools.reduce(jnp.add, [(m - mean) * (m - mean) for m in means])
    scale = lax.rsqrt(m2 * (1.0 / D) + EPS)
    out_ref[...] = (r2 - mean) * scale * own_vec[1, c] + own_vec[2, c]
    drain()


def on_device(series, emb_weight, emb_bias, q_weight, k_weight, v_weight, out_weight,
              norm1_gain, norm1_bias, ffn_in, ffn_out, norm2_gain, norm2_bias):
    vec4 = lambda a: a.reshape(4, 128)
    vm = lambda *shape: pltpu.VMEM(shape, F32)
    vb = lambda *shape: pltpu.VMEM(shape, BF16)
    block = (DH, ROWS)
    scratch = [
        vm(ROWS, 1024), vm(4, 1024, 128), vm(DH, D), vm(DH, D), vm(DH, D), vm(DH, D),
        vm(D, FF_PART), vm(FF_PART, D), vm(5, 4, 128),
        vb(8 * DH, D), vb(2 * FF_PART, D), vb(4, 256, FF_PART), vb(2 * D, D),
        vm(NC, NX, NZH, 16, D), vm(D, ROWS), vm(D, ROWS), vm(3, NC, *block),
        vm(4, NC, *block), vm(4, *block), vm(4, *block), vm(4, *block), vm(NHEAD, *block),
        vm(*block), vm(2, *block), vm(NY, *block), vm(7, 2, *block),
        vb(1024, 256), vb(256, 1024), vb(128, 1024),
        vm(NY, DH + 2, ROWS), vm(NY, DH + 2, ROWS), vm(NHEAD, *block), vm(NHEAD, *block),
        vm(4, NC, *block), vm(4, *block), vm(4, *block), vm(4, *block),
        vm(2, 2, ROWS), vm(4, 2, ROWS),
        pltpu.SemaphoreType.DMA((16,)), pltpu.SemaphoreType.DMA((COPIES,)),
        pltpu.SemaphoreType.DMA((COPIES,)), pltpu.SemaphoreType.REGULAR,
    ]
    return pl.pallas_call(
        layer_kernel,
        out_shape=jax.ShapeDtypeStruct(block, F32),
        in_specs=[pl.BlockSpec(memory_space=pl.ANY)] * 13,
        out_specs=pl.BlockSpec(memory_space=pltpu.VMEM),
        scratch_shapes=scratch,
        compiler_params=pltpu.CompilerParams(
            collective_id=0, has_side_effects=True, vmem_limit_bytes=60 * 1024 * 1024
        ),
        name="layer",
    )(series, emb_weight, vec4(emb_bias), q_weight.T, k_weight.T, v_weight.T, out_weight,
      vec4(norm1_gain), vec4(norm1_bias), ffn_in, ffn_out, vec4(norm2_gain), vec4(norm2_bias))


def solution(mesh):
    return jax.shard_map(
        on_device,
        mesh=mesh,
        in_specs=(
            P("var", "head"), P("head", None), P(), P(None, "head"), P(None, "head"),
            P(None, "head"), P("head", None), P(), P(), P(None, "head"), P("head", None), P(), P(),
        ),
        out_specs=P("head", "var"),
        check_vma=False,
    )
```

```python
import functools
import math

import jax
import jax.numpy as jnp
from jax import lax
from jax.experimental import pallas as pl
from jax.experimental.pallas import tpu as pltpu
from jax.sharding import PartitionSpec as P

MESH = pl.DeviceIdType.MESH
F32 = jnp.float32
BF16 = jnp.bfloat16

D = 512
FF_PART = 256
DH = 64
ROWS = 128
NY, NX, NZL, NZH, NC = 8, 4, 2, 4, 2
NHEAD = NZH * NC
Z_OFFS = (2, 1, 3)
Q_PAIRS = ((0, 1), (7, 2), (6, 3), (5, 4))
KV_OFFS = ((1, 0), (3, 0), (0, 1), (1, 1), (3, 1), (2, 0), (2, 1))
KV_SENDS = (7, 6, 4, 5, 3, 1, 2)
Q_SENDS = (4, 3, 5, 2, 6, 7, 1)
COPIES = 96
EPS = 1e-05


def halves(x):
    top = x.astype(BF16)
    return top, (x - top.astype(F32)).astype(BF16)


def mxu(a, b):
    return lax.dot_general(a, b, (((1,), (0,)), ((), ())), preferred_element_type=F32)


def quads(r, m, n):
    return r[:m, :n] + ((r[:m, n:] + r[m:, :n]) + r[m:, n:])


def side_by_side(x):
    return jnp.concatenate(halves(x), axis=1)


def stacked(x):
    return jnp.concatenate(halves(x), axis=0)


def column(row):
    return jnp.broadcast_to(row, (128, 128)).T


def layer_kernel(
    series_h, ew_h, eb_h, qw_h, kw_h, vw_h, ow_h, n1g_h, n1b_h, fi_h, fo_h, n2g_h, n2b_h,
    out_ref,
    series, ew, qw, kw, vw, ow, fi, fo, vec,
    wqkv, fit, fot, wot, gath, n1g, n1b, own_vec,
    epart, cbuf, sbuf, rsbuf, eown, efull, e2full,
    qsend, kvsend, qbuf, kvbuf, kst, qst, vst,
    osend, obuf, mown, mfull, normed_ref,
    fpart, fcbuf, fsbuf, frsbuf, stat, statbuf,
    lsem, ssem, rsem, own_sem,
):
    v = lax.axis_index("var")
    h = lax.axis_index("head")
    y, x, zl = v // (NX * NZL), (v // NZL) % NX, v % NZL
    zh, c = h // NC, h % NC
    oc = 1 - c

    def at(y_, x_, zl_, zh_, c_):
        return ((y_ * NX + x_) * NZL + zl_, zh_ * NC + c_)

    core_dev = at(y, x, zl, zh, oc)
    z_devs = [at(y, x, zl, (zh + off) % NZH, c) for off in Z_OFFS]
    sum_offs = (2, 1 + 2 * zl, 0, 3 - 2 * zl)
    z_order = [(zh + off) % NZH for off in sum_offs]
    sum_devs = [at(y, x, 1 - zl, zz, c) for zz in z_order]
    x_devs = [at(y, (x + off) % NX, zl, zh, c) for off in (2, 1, 3)]
    y_to = {off: at((y + off) % NY, x, zl, zh, c) for off in range(1, NY)}
    y_from = {off: at((y + NY - off) % NY, x, zl, zh, c) for off in range(1, NY)}
    kv_devs = [at(y, (x + dx) % NX, (zl + dz) % NZL, zh, c) for dx, dz in KV_OFFS]

    count = [0]
    pending = []

    def send(src, dst, dev):
        i = count[0]
        count[0] += 1
        cp = pltpu.make_async_remote_copy(
            src_ref=src, dst_ref=dst, send_sem=ssem.at[i], recv_sem=rsem.at[i],
            device_id=dev, device_id_type=MESH,
        )
        cp.start()
        pending.append(cp)
        return cp

    def drain(keep=0):
        while len(pending) > keep:
            pending.pop(0).wait_send()

    def fence():
        pl.semaphore_signal(own_sem, 1)
        pl.semaphore_wait(own_sem, 1)

    lcount = [0]

    def load(src, dst):
        i = lcount[0]
        lcount[0] += 1
        cp = pltpu.make_async_copy(src, dst, lsem.at[i])
        cp.start()
        return cp

    ld_series = load(series_h, series)

    def load_ew(k):
        cols = pl.ds(pl.multiple_of(z_order[k] * 128, 128), 128)
        return load(ew_h.at[:, cols], ew.at[k])

    ld_ew = [load_ew(0)]
    barrier = pltpu.get_barrier_semaphore()
    greeted = z_devs + [core_dev] + sum_devs[:2] + sum_devs[3:] + [y_to[off] for off in range(1, NY)] + kv_devs
    for dev in greeted:
        pl.semaphore_signal(barrier, inc=1, device_id=dev, device_id_type=MESH)
    ld_ew += [load_ew(k) for k in (1, 2, 3)]

    ld_series.wait()
    s_stack = stacked(series[...])

    def emb_step(k):
        ld_ew[k].wait()
        r = mxu(s_stack, side_by_side(ew[k]))
        epart[k] = quads(r, ROWS, 128).T.reshape(NC, DH, ROWS)

    emb_step(0)
    ld_ow = load(ow_h, ow)
    ld_vec = [load(r, vec.at[i]) for i, r in enumerate((eb_h, n1g_h, n1b_h, n2g_h, n2b_h))]
    ld_qkv = [load(a, b) for a, b in ((qw_h, qw), (kw_h, kw), (vw_h, vw))]
    ld_ffn = [load(a, b) for a, b in ((fi_h, fi), (fo_h, fo))]
    pl.semaphore_wait(barrier, len(greeted))

    core_cps = [send(epart.at[0, oc], cbuf.at[0], core_dev)]
    fence()
    emb_step(1)
    core_cps.append(send(epart.at[1, oc], cbuf.at[1], core_dev))
    fence()
    z_cps = []

    def to_chip(k):
        core_cps[k].wait_recv()
        sbuf[k] = epart[k, c] + cbuf[k]
        z_cps.append(send(sbuf.at[k], rsbuf.at[k], sum_devs[k]))

    to_chip(0)
    emb_step(2)
    core_cps.append(send(epart.at[2, oc], cbuf.at[2], core_dev))
    fence()
    to_chip(1)
    emb_step(3)
    core_cps.append(send(epart.at[3, oc], cbuf.at[3], core_dev))
    fence()
    to_chip(2)
    to_chip(3)

    ld_ow.wait()
    xrows = pl.ds(pl.multiple_of(x * 16, 16), 16)
    gath[c, x, zh] = ow[xrows, :]
    w_z = [send(gath.at[c, x, zh], gath.at[c, x, zh], dev) for dev in z_devs]
    fence()

    for ld in ld_vec + ld_qkv:
        ld.wait()
    kt = kw[...]
    wqkv[...] = stacked(jnp.concatenate([qw[...], vw[...], kt, kt], axis=0))
    for i, j in enumerate((0, 3, 4)):
        own_vec[i] = column(vec[j, pl.ds(zh, 1), :]).reshape(NC, DH, ROWS)

    for cp in z_cps:
        cp.wait_recv()
    eown[...] = (rsbuf[0] + rsbuf[1]) + (rsbuf[2] + rsbuf[3]) + own_vec[0, c]

    def start_gather(block, full):
        return [send(block, full.at[h], dev) for dev in sum_devs]

    def share_gather(zs, full):
        cs = []
        for k in (2, 3, 1, 0):
            zs[k].wait_recv()
            off = (2, 3 - 2 * zl, 0, 1 + 2 * zl)[k]
            hs = ((zh + NZH - off) % NZH) * NC + c
            cs.append(send(full.at[hs], full.at[hs], core_dev))
        return cs

    def gather_heads(block, full, meanwhile):
        zs = start_gather(block, full)
        fence()
        drain(keep=4)
        meanwhile()
        for cp in share_gather(zs, full):
            cp.wait_recv()

    def prepare_ffn_in():
        for cp in w_z:
            cp.wait_recv()
        ld_ffn[0].wait()
        fit[...] = stacked(fi[...].T)

    gather_heads(eown, efull, prepare_ffn_in)

    emb_t = efull[...].reshape(D, ROWS)
    qkv = quads(mxu(wqkv[...], side_by_side(emb_t)), 4 * DH, ROWS)
    qsend[...] = qkv[:DH] * (math.log2(math.e) / math.sqrt(DH))
    kk = qkv[2 * DH :].T
    left = lax.broadcasted_iota(jnp.int32, (DH, 128), 1) < DH
    kvsend[0] = jnp.where(left, kk[:DH], kk[DH:])
    kvsend[1] = qkv[DH : 2 * DH]

    q_cps, kv_cps = {}, {}

    def send_kv(*slots):
        for i in slots:
            kv_cps[i] = send(kvsend, kvbuf.at[i - 1], kv_devs[i - 1])

    def send_q(*slots):
        for off in slots:
            q_cps[off] = send(qsend, qbuf.at[off], y_to[off])

    for i, off in zip(KV_SENDS, Q_SENDS):
        send_kv(i)
        send_q(off)
    fence()
    drain(keep=14)

    ld_ffn[1].wait()
    for z in range(NZH):
        fot[z] = stacked(fo[:, z * 128 : (z + 1) * 128].T)
        n1g[pl.ds(z * 128, 128), :] = column(vec[1, z : z + 1, :])
        n1b[pl.ds(z * 128, 128), :] = column(vec[2, z : z + 1, :])
    def put_key(i, pack):
        other = pltpu.roll(pack, DH, 1)
        for j, kd in enumerate((jnp.where(left, pack, other), jnp.where(left, other, pack))):
            top, rest = halves(kd)
            rows = slice(i * ROWS + j * DH, i * ROWS + (j + 1) * DH)
            kst[rows, :128] = top
            kst[rows, 128:] = rest

    def put_query(j, qt):
        top, rest = halves(qt)
        cols = slice(j * ROWS, (j + 1) * ROWS)
        for r in range(2):
            qst[2 * r * DH : (2 * r + 1) * DH, cols] = top
            qst[(2 * r + 1) * DH : (2 * r + 2) * DH, cols] = rest

    def put_value(i, vt):
        vst[:, i * ROWS : (i + 1) * ROWS] = stacked(vt)

    def put_kv(i):
        kv = kvbuf.at[i - 1] if i else kvsend
        put_key(i, kv[0])
        put_value(i, kv[1])

    put_kv(0)
    put_query(0, qsend[...])
    places = {off: 2 * pair + j for pair in range(4) for j, off in enumerate(Q_PAIRS[pair])}
    for i, off in zip(KV_SENDS, Q_SENDS):
        kv_cps[i].wait_recv()
        put_kv(i)
        q_cps[off].wait_recv()
        put_query(places[off], qbuf[off])

    o_cps = {}
    for pair in (3, 2, 1, 0):
        s = mxu(kst[...], qst[:, 2 * pair * ROWS : (2 * pair + 2) * ROWS])
        top_score = jnp.max(s, axis=0, keepdims=True)
        p = jnp.exp2(s - top_score)
        total = jnp.sum(p, axis=0, keepdims=True)
        p_top, p_rest = halves(p)
        o = mxu(vst[...], p_top) + mxu(vst[...], p_rest)
        o = o[:DH] + o[DH:]
        for j in (1, 0):
            off = Q_PAIRS[pair][j]
            cols = slice(j * ROWS, (j + 1) * ROWS)
            osend[off, :DH] = o[:, cols]
            osend[off, DH : DH + 1] = top_score[:, cols]
            osend[off, DH + 1 : DH + 2] = total[:, cols]
            if off:
                o_cps[off] = send(osend.at[off], obuf.at[off], y_from[off])
        if pair:
            fence()

    w_x = [send(gath.at[c, x], gath.at[c, x], dev) for dev in x_devs]
    e_cps = start_gather(efull.at[h], e2full)
    drain(keep=14)

    def prepare_out_weight():
        for cp in w_x:
            cp.wait_recv()
        send(gath.at[c], gath.at[c], core_dev).wait_recv()
        for z in range(NZH):
            block = jnp.concatenate(
                [gath[par, xx, z] for par in range(NC) for xx in range(NX)], axis=0
            )
            top, rest = halves(block.T)
            wot[:D, z * 128 : (z + 1) * 128] = top
            wot[D:, z * 128 : (z + 1) * 128] = rest

    e_shared = share_gather(e_cps, e2full)

    for off in range(1, NY):
        o_cps[off].wait_recv()
    tops = [osend[0, DH : DH + 1]] + [obuf[off, DH : DH + 1] for off in range(1, NY)]
    best = functools.reduce(jnp.maximum, tops)
    scales = [jnp.exp2(t - best) for t in tops]
    denom = scales[0] * osend[0, DH + 1 : DH + 2]
    acc = scales[0] * osend[0, :DH]
    for off in range(1, NY):
        denom += scales[off] * obuf[off, DH + 1 : DH + 2]
        acc += scales[off] * obuf[off, :DH]
    mown[...] = acc / denom

    gather_heads(mown, mfull, prepare_out_weight)
    for cp in e_shared:
        cp.wait_recv()

    mixed_t = mfull[...].reshape(D, ROWS)
    resid = e2full[...].reshape(D, ROWS) + quads(mxu(wot[...], side_by_side(mixed_t)), D, ROWS)
    centre = jnp.sum(resid, axis=0, keepdims=True) * (1.0 / D)
    spread = resid - centre
    variance = jnp.sum(spread * spread, axis=0, keepdims=True) * (1.0 / D)
    normed = spread * lax.rsqrt(variance + EPS) * n1g[...] + n1b[...]
    normed_ref[...] = normed.reshape(NHEAD, DH, ROWS)
    hid = quads(mxu(fit[...], side_by_side(normed)), FF_PART, ROWS)
    hid = hid * (1.0 + lax.erf(hid * (1.0 / math.sqrt(2.0)))) * 0.5
    hid2 = side_by_side(hid)

    fcore = []
    for k in range(4):
        fpart[k] = quads(mxu(fot[z_order[k]], hid2), 128, ROWS).reshape(NC, DH, ROWS)
        fcore.append(send(fpart.at[k, oc], fcbuf.at[k], core_dev))
        fence()
    fz = []
    for k in range(4):
        fcore[k].wait_recv()
        chip_sum = fpart[k, c] + fcbuf[k]
        fsbuf[k] = chip_sum + normed_ref[h] if k == 2 else chip_sum
        fz.append(send(fsbuf.at[k], frsbuf.at[k], sum_devs[k]))
    drain(keep=8)
    for cp in fz:
        cp.wait_recv()
    r2 = (frsbuf[0] + frsbuf[1]) + (frsbuf[2] + frsbuf[3])

    mean_own = jnp.sum(r2, axis=0, keepdims=True) * (1.0 / DH)
    dev_own = r2 - mean_own
    m2_own = jnp.sum(dev_own * dev_own, axis=0, keepdims=True)
    stat[0, 0:1] = mean_own
    stat[0, 1:2] = m2_own
    send(stat.at[0], statbuf.at[3], core_dev).wait_recv()
    gap = mean_own - statbuf[3, 0:1]
    mean_pair = 0.5 * (mean_own + statbuf[3, 0:1])
    m2_pair = m2_own + statbuf[3, 1:2] + (0.5 * DH) * gap * gap
    stat[1, 0:1] = mean_pair
    stat[1, 1:2] = m2_pair
    st = [send(stat.at[1], statbuf.at[i], dev) for i, dev in enumerate(z_devs)]
    drain(keep=3)
    for cp in st:
        cp.wait_recv()
    means = [mean_pair] + [statbuf[i, 0:1] for i in range(3)]
    mean = functools.reduce(jnp.add, means) * (1.0 / NZH)
    m2 = functools.reduce(jnp.add, [m2_pair] + [statbuf[i, 1:2] for i in range(3)])
    m2 += 2 * DH * functools.reduce(jnp.add, [(m - mean) * (m - mean) for m in means])
    scale = lax.rsqrt(m2 * (1.0 / D) + EPS)
    out_ref[...] = (r2 - mean) * scale * own_vec[1, c] + own_vec[2, c]
    drain()


def on_device(series, emb_weight, emb_bias, q_weight, k_weight, v_weight, out_weight,
              norm1_gain, norm1_bias, ffn_in, ffn_out, norm2_gain, norm2_bias):
    vec4 = lambda a: a.reshape(4, 128)
    vm = lambda *shape: pltpu.VMEM(shape, F32)
    vb = lambda *shape: pltpu.VMEM(shape, BF16)
    block = (DH, ROWS)
    scratch = [
        vm(ROWS, 1024), vm(4, 1024, 128), vm(DH, D), vm(DH, D), vm(DH, D), vm(DH, D),
        vm(D, FF_PART), vm(FF_PART, D), vm(5, 4, 128),
        vb(8 * DH, D), vb(2 * FF_PART, D), vb(4, 256, FF_PART), vb(2 * D, D),
        vm(NC, NX, NZH, 16, D), vm(D, ROWS), vm(D, ROWS), vm(3, NC, *block),
        vm(4, NC, *block), vm(4, *block), vm(4, *block), vm(4, *block), vm(*block),
        vm(NHEAD, *block), vm(NHEAD, *block),
        vm(*block), vm(2, *block), vm(NY, *block), vm(7, 2, *block),
        vb(1024, 256), vb(256, 1024), vb(128, 1024),
        vm(NY, DH + 2, ROWS), vm(NY, DH + 2, ROWS), vm(*block), vm(NHEAD, *block), vm(NHEAD, *block),
        vm(4, NC, *block), vm(4, *block), vm(4, *block), vm(4, *block),
        vm(2, 2, ROWS), vm(4, 2, ROWS),
        pltpu.SemaphoreType.DMA((16,)), pltpu.SemaphoreType.DMA((COPIES,)),
        pltpu.SemaphoreType.DMA((COPIES,)), pltpu.SemaphoreType.REGULAR,
    ]
    return pl.pallas_call(
        layer_kernel,
        out_shape=jax.ShapeDtypeStruct(block, F32),
        in_specs=[pl.BlockSpec(memory_space=pl.ANY)] * 13,
        out_specs=pl.BlockSpec(memory_space=pltpu.VMEM),
        scratch_shapes=scratch,
        compiler_params=pltpu.CompilerParams(
            collective_id=0, has_side_effects=True, vmem_limit_bytes=60 * 1024 * 1024
        ),
        name="layer",
    )(series, emb_weight, vec4(emb_bias), q_weight.T, k_weight.T, v_weight.T, out_weight,
      vec4(norm1_gain), vec4(norm1_bias), ffn_in, ffn_out, vec4(norm2_gain), vec4(norm2_bias))


def solution(mesh):
    return jax.shard_map(
        on_device,
        mesh=mesh,
        in_specs=(
            P("var", "head"), P("head", None), P(), P(None, "head"), P(None, "head"),
            P(None, "head"), P("head", None), P(), P(), P(None, "head"), P("head", None), P(), P(),
        ),
        out_specs=P("head", "var"),
        check_vma=False,
    )
```
